32 devices in a mesh: row: 4 (over y, x), col: 8 (over z, core).
Axes of the slice: x: 2, y: 2, z: 4, core: 2. Of those that a mesh axis runs over, the one named last changes fastest.
Arguments:
- state: float32 [3072, 3072], P('col', 'row'), may hold values from -300 to 300
- noise: float32 [3072, 3072], P('col', 'row'), may hold values from -6 to 6
- mod_shift: float32 [3072], P('col'), may hold values from -3 to 3
- mod_scale: float32 [3072], P('col'), may hold values from -2.5 to 2.5
- mod_gate: float32 [3072], P('col'), may hold values from 0.3 to 3
- w_in: bfloat16 [3072, 12288], P('row', 'col'), may hold values from -0.109375 to 0.109375
- b_in: float32 [12288], P('col'), may hold values from -3 to 3
- w_out: bfloat16 [3072, 12288], P('col', 'row'), may hold values from -0.0546875 to 0.0546875
- b_out: float32 [3072], P('col'), may hold values from -2.5 to 2.5
Outputs:
- purified: float32 [3072, 3072], P('col', 'row')
- predicted: float32 [3072, 3072], P('col', 'row')
The draws below stay inside these ranges and needn't reach their ends.
All inputs are finite; a program needn't handle non-finite values.
Results may differ from the reference program's by a relative error of at most 0.00049.
Values may be sent and summed in bfloat16 or wider, within the bound.
A program may use at most 128 MiB of HBM per device.

```python
import math
import jax
import jax.numpy as jnp
from jax import lax

D = 3072
FF = 12288
TOKENS = 3072


def draw_state(key, part):
    key_base, key_feat, key_rows = jax.random.split(key, 3)
    position = jnp.arange(D, dtype=jnp.float32) / D
    rough = jax.random.uniform(key_feat, (D,), jnp.float32, -0.4, 0.4)
    token_level = jax.random.uniform(key_rows, (1, TOKENS), jnp.float32, 0.0, math.log(10.0))
    base = jnp.clip(jax.random.normal(key_base, (D, TOKENS), jnp.float32), -6.0, 6.0)
    feature = jnp.exp(math.log(3.0) * position + rough)
    return base * jnp.exp(token_level) * feature[:, None]


def block_scale(own_key, extent, pieces, smallest, high):
    def one(dim, parts):
        heights = jax.random.uniform(jax.random.fold_in(jax.random.fold_in(own_key, 6), dim), (parts,), jnp.float32, smallest / len(pieces), high / len(pieces))
        return jnp.repeat(jnp.exp(heights), extent[dim] // parts).reshape((-1,) + (1,) * (len(extent) - dim - 1))

    factor_of = one(*pieces[0])
    for cut in pieces[1:]:
        factor_of = factor_of * one(*cut)
    return factor_of


def centred(own_key, extent, scale, reach, cuts=(), kind=jnp.bfloat16):
    gain = block_scale(own_key, extent, cuts, -0.22, 0.18) if cuts else 1.0
    array = jax.random.normal(own_key, extent, jnp.float32) * scale * gain
    return jnp.minimum(jnp.maximum(array, -reach), reach).astype(kind)


def setup_inputs(seed: int = 0) -> dict:
    keys = jax.random.split(jax.random.key(seed), 10)
    return {
        "state": draw_state(jax.random.fold_in(keys[9], 71), 0),
        "noise": centred(keys[1], (D, TOKENS), 1.0, 6.0, ((0, 8), (1, 4)), jnp.float32),
        "mod_shift": centred(keys[2], (D,), 0.5, 3.0, ((0, 8),), jnp.float32),
        "mod_scale": centred(keys[3], (D,), 0.3, 2.5, ((0, 8),), jnp.float32),
        "mod_gate": jnp.clip(jnp.exp(math.log(3.0) - 2.3025851 * jax.random.uniform(keys[4], (D,), jnp.float32) ** block_scale(keys[4], (D,), ((0, 8),), -0.2, 0.2)), 0.3, 3.0),
        "w_in": centred(keys[5], (D, FF), D ** -0.5, 0.109375, ((0, 4), (1, 8))),
        "b_in": centred(keys[6], (FF,), 0.5, 3.0, ((0, 8),), jnp.float32),
        "w_out": centred(keys[7], (D, FF), FF ** -0.5, 0.0546875, ((0, 8), (1, 4))),
        "b_out": centred(keys[8], (D,), 0.3, 2.5, ((0, 8),), jnp.float32),
    }


beta_now = 2.09
step_width = 0.02
sigma_now = 0.322

def reference(state, noise, mod_shift, mod_scale, mod_gate, w_in, b_in, w_out, b_out):
    center = lax.optimization_barrier(jnp.sum(state, axis=0)) / D
    spread = lax.optimization_barrier(jnp.sum(state * state, axis=0)) / D - center * center
    normed = ((state - center[None, :]) * jax.lax.rsqrt(spread[None, :] + 1e-06) * (1.0 + mod_scale[:, None]) + mod_shift[:, None]).astype(jnp.bfloat16)
    pre_act = jax.lax.dot_general(w_in, normed, (((0,), (0,)), ((), ())), preferred_element_type=jnp.float32) + b_in[:, None]
    hidden = jax.nn.gelu(pre_act, approximate=True).astype(jnp.bfloat16)
    branch = jnp.dot(w_out, hidden, preferred_element_type=jnp.float32) + b_out[:, None]
    predicted = state + mod_gate[:, None] * branch
    purified = state * (1.0 + 0.5 * beta_now * step_width) - beta_now * step_width / sigma_now * predicted + math.sqrt(beta_now * step_width) * noise
    return (purified, predicted)
```

```python
import math

import jax
import jax.numpy as jnp
from jax import lax
from jax.sharding import PartitionSpec as P

D = 3072


beta_now = 2.09
step_width = 0.02
sigma_now = 0.322


def on_device(state, noise, mod_shift, mod_scale, mod_gate, w_in, b_in, w_out, b_out):
    w_in_all = lax.all_gather(w_in, "row", axis=0, tiled=True)
    w_out_all = lax.all_gather(w_out, "row", axis=1, tiled=True)
    col_sums, squares = lax.psum((jnp.sum(state, axis=0), jnp.sum(state * state, axis=0)), "col")
    center = col_sums / D
    spread = squares / D - center * center
    normed = (
        (state - center[None, :]) * lax.rsqrt(spread[None, :] + 1e-06) * (1.0 + mod_scale[:, None])
        + mod_shift[:, None]
    ).astype(jnp.bfloat16)
    normed_all = lax.all_gather(normed, "col", axis=0, tiled=True)
    pre_act = lax.dot_general(
        w_in_all, normed_all, (((0,), (0,)), ((), ())), preferred_element_type=jnp.float32
    )
    hidden = jax.nn.gelu(pre_act + b_in[:, None], approximate=True).astype(jnp.bfloat16)
    hidden_all = lax.all_gather(hidden, "col", axis=0, tiled=True)
    mixed_out = jnp.dot(w_out_all, hidden_all, preferred_element_type=jnp.float32)
    branch = mixed_out + b_out[:, None]
    predicted = state + mod_gate[:, None] * branch
    purified = (
        state * (1.0 + 0.5 * beta_now * step_width)
        - beta_now * step_width / sigma_now * predicted
        + math.sqrt(beta_now * step_width) * noise
    )
    return (purified, predicted)


def solution(mesh):
    in_specs = (
        P("col", "row"),
        P("col", "row"),
        P("col"),
        P("col"),
        P("col"),
        P("row", "col"),
        P("col"),
        P("col", "row"),
        P("col"),
    )
    out_specs = (P("col", "row"), P("col", "row"))
    return jax.shard_map(
        on_device, mesh=mesh, in_specs=in_specs, out_specs=out_specs, check_vma=False
    )
```

```python
import math

import jax
import jax.numpy as jnp
from jax import lax
from jax.sharding import PartitionSpec as P

D = 3072


beta_now = 2.09
step_width = 0.02
sigma_now = 0.322


def flipped(value, axis, bits):
    devices = lax.axis_size(axis)
    return lax.ppermute(value, axis, [(i, i ^ bits) for i in range(devices)])


def spread_blocks(block, dim, axis):
    half = block.shape[dim] // 2
    held = {0: block}
    pieces = {0: [(0, block)]}
    order = sorted(range(1, lax.axis_size(axis)), key=lambda k: (k.bit_count(), k))
    for k in order:
        low = k & -k
        high = 1 << (k.bit_length() - 1)
        if low == high:
            held[k] = flipped(block, axis, k)
            pieces[k] = [(0, held[k])]
        else:
            first = lax.slice_in_dim(held[k ^ low], 0, half, axis=dim)
            second = lax.slice_in_dim(held[k ^ high], half, 2 * half, axis=dim)
            first, second = flipped(first, axis, low), flipped(second, axis, high)
            pieces[k] = [(0, first), (half, second)]
            if k.bit_count() < lax.axis_size(axis).bit_length() - 1:
                held[k] = lax.concatenate([first, second], dim)
    return pieces, held


def on_device(state, noise, mod_shift, mod_scale, mod_gate, w_in, b_in, w_out, b_out):
    row = lax.axis_index("row")
    in_pieces, in_held = spread_blocks(w_in, 0, "row")
    w_out, _ = lax.optimization_barrier((w_out, in_held[1]))
    out_pieces, _ = spread_blocks(w_out, 1, "row")
    col_sums, squares = lax.psum((jnp.sum(state, axis=0), jnp.sum(state * state, axis=0)), "col")
    center = col_sums / D
    spread = squares / D - center * center
    normed = (
        (state - center[None, :]) * lax.rsqrt(spread[None, :] + 1e-06) * (1.0 + mod_scale[:, None])
        + mod_shift[:, None]
    ).astype(jnp.bfloat16)
    normed_all = lax.all_gather(normed, "col", axis=0, tiled=True)
    tokens = state.shape[1]
    chunk = tokens // 3 if tokens % 384 == 0 else tokens
    spans = [(lo, lo + chunk) for lo in range(0, tokens, chunk)]

    gathered = []
    for lo, hi in spans:
        pre_act = None
        for k, parts in in_pieces.items():
            for offset, piece in parts:
                start = (row ^ k) * w_in.shape[0] + offset
                part = lax.dynamic_slice(normed_all, (start, lo), (piece.shape[0], hi - lo))
                term = lax.dot_general(
                    piece, part, (((0,), (0,)), ((), ())), preferred_element_type=jnp.float32
                )
                pre_act = term if pre_act is None else pre_act + term
        hidden = jax.nn.gelu(pre_act + b_in[:, None], approximate=True).astype(jnp.bfloat16)
        gathered.append(lax.all_gather(hidden, "col", axis=0, tiled=True))

    outs = []
    for (lo, hi), hidden_all in zip(spans, gathered):
        mixed_out = None
        for k, parts in out_pieces.items():
            for offset, piece in parts:
                start = (row ^ k) * w_out.shape[1] + offset
                part = lax.dynamic_slice(hidden_all, (start, 0), (piece.shape[1], hi - lo))
                term = jnp.dot(piece, part, preferred_element_type=jnp.float32)
                mixed_out = term if mixed_out is None else mixed_out + term
        branch = mixed_out + b_out[:, None]
        now = state[:, lo:hi]
        predicted = now + mod_gate[:, None] * branch
        purified = (
            now * (1.0 + 0.5 * beta_now * step_width)
            - beta_now * step_width / sigma_now * predicted
            + math.sqrt(beta_now * step_width) * noise[:, lo:hi]
        )
        outs.append((purified, predicted))
    return tuple(lax.concatenate(list(parts), 1) for parts in zip(*outs))


def solution(mesh):
    in_specs = (
        P("col", "row"),
        P("col", "row"),
        P("col"),
        P("col"),
        P("col"),
        P("row", "col"),
        P("col"),
        P("col", "row"),
        P("col"),
    )
    out_specs = (P("col", "row"), P("col", "row"))
    return jax.shard_map(
        on_device, mesh=mesh, in_specs=in_specs, out_specs=out_specs, check_vma=False
    )
```

```python
import math

import jax
import jax.numpy as jnp
from jax import lax
from jax.sharding import PartitionSpec as P

D = 3072


beta_now = 2.09
step_width = 0.02
sigma_now = 0.322


def flipped(value, axis, bits):
    devices = lax.axis_size(axis)
    return lax.ppermute(value, axis, [(i, i ^ bits) for i in range(devices)])


def spread_blocks(block, dim, axis):
    half = block.shape[dim] // 2
    held = {0: block}
    pieces = {0: [(0, block)]}
    order = sorted(range(1, lax.axis_size(axis)), key=lambda k: (k.bit_count(), k))
    for k in order:
        low = k & -k
        high = 1 << (k.bit_length() - 1)
        if low == high:
            held[k] = flipped(block, axis, k)
            pieces[k] = [(0, held[k])]
        else:
            first = lax.slice_in_dim(held[k ^ low], 0, half, axis=dim)
            second = lax.slice_in_dim(held[k ^ high], half, 2 * half, axis=dim)
            first, second = flipped(first, axis, low), flipped(second, axis, high)
            pieces[k] = [(0, first), (half, second)]
            if k.bit_count() < lax.axis_size(axis).bit_length() - 1:
                held[k] = lax.concatenate([first, second], dim)
    return pieces, held


def chain_step(value, moves):
    return lax.ppermute(
        value, "col", [(2 * a + core, 2 * b + core) for a, b in moves for core in range(2)]
    )


def gather_chain(hidden):
    chips = lax.axis_size("col") // 2
    chip = lax.axis_index("col") // 2
    blocks = [(chip, hidden)]
    upward = downward = hidden
    for step in range(1, chips):
        up = [(a, a + 1) for a in range(step - 1, chips - 1)]
        down = [(a, a - 1) for a in range(1, chips - step + 1)]
        if 2 * step > chips + 1:
            upward = downward = chain_step(upward, up + down)
        else:
            upward, downward = chain_step(upward, up), chain_step(downward, down)
            if 2 * step > chips - 1:
                upward = downward = jnp.where(chip >= step, upward, downward)
        if 2 * step > chips - 1:
            blocks.append((jnp.where(chip >= step, chip - step, jnp.minimum(chip + step, chips - 1)), upward))
        else:
            blocks.append((jnp.maximum(chip - step, 0), upward))
            blocks.append((jnp.minimum(chip + step, chips - 1), downward))
    return blocks


def on_device(state, noise, mod_shift, mod_scale, mod_gate, w_in, b_in, w_out, b_out):
    row = lax.axis_index("row")
    core = lax.axis_index("col") % 2
    in_pieces, _ = spread_blocks(w_in, 0, "row")
    sums = jnp.stack((jnp.sum(state, axis=0), jnp.sum(state * state, axis=0)))
    bits = 1
    while bits < lax.axis_size("col"):
        sums = sums + flipped(sums, "col", bits)
        bits *= 2
    center = sums[0] / D
    spread = sums[1] / D - center * center
    normed = (
        (state - center[None, :]) * lax.rsqrt(spread[None, :] + 1e-06) * (1.0 + mod_scale[:, None])
        + mod_shift[:, None]
    ).astype(jnp.bfloat16)
    normed_all = lax.all_gather(normed, "col", axis=0, tiled=True)

    pre_act = None
    for k, parts in in_pieces.items():
        for offset, piece in parts:
            start = (row ^ k) * w_in.shape[0] + offset
            part = lax.dynamic_slice_in_dim(normed_all, start, piece.shape[0], axis=0)
            term = lax.dot_general(
                piece, part, (((0,), (0,)), ((), ())), preferred_element_type=jnp.float32
            )
            pre_act = term if pre_act is None else pre_act + term
    hidden = jax.nn.gelu(pre_act + b_in[:, None], approximate=True).astype(jnp.bfloat16)
    last = list(in_pieces.values())[-1]
    w_out, *_ = lax.optimization_barrier((w_out, *[piece for _, piece in last]))
    w_out_all = lax.all_gather(w_out, "row", axis=1, tiled=True)

    mixed_out = None
    units = w_in.shape[1]
    for owner, block in gather_chain(hidden):
        for near, value in ((core, block), (1 - core, flipped(block, "col", 1))):
            weights = lax.dynamic_slice_in_dim(w_out_all, (2 * owner + near) * units, units, axis=1)
            term = jnp.dot(weights, value, preferred_element_type=jnp.float32)
            mixed_out = term if mixed_out is None else mixed_out + term
    branch = mixed_out + b_out[:, None]
    predicted = state + mod_gate[:, None] * branch
    purified = (
        state * (1.0 + 0.5 * beta_now * step_width)
        - beta_now * step_width / sigma_now * predicted
        + math.sqrt(beta_now * step_width) * noise
    )
    return (purified, predicted)


def solution(mesh):
    in_specs = (
        P("col", "row"),
        P("col", "row"),
        P("col"),
        P("col"),
        P("col"),
        P("row", "col"),
        P("col"),
        P("col", "row"),
        P("col"),
    )
    out_specs = (P("col", "row"), P("col", "row"))
    return jax.shard_map(
        on_device, mesh=mesh, in_specs=in_specs, out_specs=out_specs, check_vma=False
    )
```

```python
import math

import jax
import jax.numpy as jnp
from jax import lax
from jax.sharding import PartitionSpec as P

D = 3072


beta_now = 2.09
step_width = 0.02
sigma_now = 0.322


def flipped(value, axis, bits):
    devices = lax.axis_size(axis)
    return lax.ppermute(value, axis, [(i, i ^ bits) for i in range(devices)])


def spread_blocks(block, dim, axis):
    half = block.shape[dim] // 2
    held = {0: block}
    pieces = {0: [(0, block)]}
    order = sorted(range(1, lax.axis_size(axis)), key=lambda k: (k.bit_count(), k))
    for k in order:
        low = k & -k
        high = 1 << (k.bit_length() - 1)
        if low == high:
            held[k] = flipped(block, axis, k)
            pieces[k] = [(0, held[k])]
        else:
            first = lax.slice_in_dim(held[k ^ low], 0, half, axis=dim)
            second = lax.slice_in_dim(held[k ^ high], half, 2 * half, axis=dim)
            first, second = flipped(first, axis, low), flipped(second, axis, high)
            pieces[k] = [(0, first), (half, second)]
            if k.bit_count() < lax.axis_size(axis).bit_length() - 1:
                held[k] = lax.concatenate([first, second], dim)
    return pieces, held


def chain_step(value, moves):
    return lax.ppermute(
        value, "col", [(2 * a + core, 2 * b + core) for a, b in moves for core in range(2)]
    )


def gather_chain(hidden):
    chips = lax.axis_size("col") // 2
    chip = lax.axis_index("col") // 2
    blocks = [(chip, hidden, flipped(hidden, "col", 1))]
    upward = downward = hidden
    for step in range(1, chips):
        up = [(a, a + 1) for a in range(step - 1, chips - 1)]
        down = [(a, a - 1) for a in range(1, chips - step + 1)]
        if 2 * step > chips + 1:
            owns, mains, others = zip(*blocks)
            swapped = others[: -1]
            upward, *swapped = lax.optimization_barrier((upward, *swapped))
            blocks = list(zip(owns, mains, [*swapped, *others[-1:]]))
            upward = downward = chain_step(upward, up + down)
        else:
            upward, downward = chain_step(upward, up), chain_step(downward, down)
            if 2 * step > chips - 1:
                upward = downward = jnp.where(chip >= step, upward, downward)
        if 2 * step > chips - 1:
            owner = jnp.where(chip >= step, chip - step, jnp.minimum(chip + step, chips - 1))
            swapped = flipped(upward, "col", 1) if step < chips - 1 else None
            blocks.append((owner, upward, swapped))
        else:
            for owner, block in ((chip - step, upward), (chip + step, downward)):
                swapped = flipped(block, "col", 1) if step < chips - 1 else None
                blocks.append((jnp.clip(owner, 0, chips - 1), block, swapped))
    return blocks


def on_device(state, noise, mod_shift, mod_scale, mod_gate, w_in, b_in, w_out, b_out):
    row = lax.axis_index("row")
    core = lax.axis_index("col") % 2
    in_pieces, _ = spread_blocks(w_in, 0, "row")
    sums = jnp.stack((jnp.sum(state, axis=0), jnp.sum(state * state, axis=0)))
    bits = 1
    while bits < lax.axis_size("col"):
        sums = sums + flipped(sums, "col", bits)
        bits *= 2
    center = sums[0] / D
    spread = sums[1] / D - center * center
    normed = (
        (state - center[None, :]) * lax.rsqrt(spread[None, :] + 1e-06) * (1.0 + mod_scale[:, None])
        + mod_shift[:, None]
    ).astype(jnp.bfloat16)
    normed_all = lax.all_gather(normed, "col", axis=0, tiled=True)

    pre_act = None
    for k, parts in in_pieces.items():
        if k and len(parts) > 1:
            pre_act, *arrived = lax.optimization_barrier((pre_act, *[piece for _, piece in parts]))
            parts = [(offset, piece) for (offset, _), piece in zip(parts, arrived)]
        for offset, piece in parts:
            start = (row ^ k) * w_in.shape[0] + offset
            part = lax.dynamic_slice_in_dim(normed_all, start, piece.shape[0], axis=0)
            term = lax.dot_general(
                piece, part, (((0,), (0,)), ((), ())), preferred_element_type=jnp.float32
            )
            pre_act = term if pre_act is None else pre_act + term
    hidden = jax.nn.gelu(pre_act + b_in[:, None], approximate=True).astype(jnp.bfloat16)
    w_out, _ = lax.optimization_barrier((w_out, piece))
    w_out_all = lax.all_gather(w_out, "row", axis=1, tiled=True)

    mixed_out = None
    units = w_in.shape[1]
    blocks = gather_chain(hidden)
    for owner, block, swapped in blocks:
        if swapped is None:
            block, mixed_out = lax.optimization_barrier((block, mixed_out))
            swapped = flipped(block, "col", 1)
        for near, value in ((core, block), (1 - core, swapped)):
            weights = lax.dynamic_slice_in_dim(w_out_all, (2 * owner + near) * units, units, axis=1)
            term = jnp.dot(weights, value, preferred_element_type=jnp.float32)
            mixed_out = term if mixed_out is None else mixed_out + term
    branch = mixed_out + b_out[:, None]
    predicted = state + mod_gate[:, None] * branch
    purified = (
        state * (1.0 + 0.5 * beta_now * step_width)
        - beta_now * step_width / sigma_now * predicted
        + math.sqrt(beta_now * step_width) * noise
    )
    return (purified, predicted)


def solution(mesh):
    in_specs = (
        P("col", "row"),
        P("col", "row"),
        P("col"),
        P("col"),
        P("col"),
        P("row", "col"),
        P("col"),
        P("col", "row"),
        P("col"),
    )
    out_specs = (P("col", "row"), P("col", "row"))
    return jax.shard_map(
        on_device, mesh=mesh, in_specs=in_specs, out_specs=out_specs, check_vma=False
    )
```

```python
import math

import jax
import jax.numpy as jnp
from jax import lax
from jax.sharding import PartitionSpec as P

D = 3072


beta_now = 2.09
step_width = 0.02
sigma_now = 0.322


def flipped(value, axis, bits):
    devices = lax.axis_size(axis)
    return lax.ppermute(value, axis, [(i, i ^ bits) for i in range(devices)])


def spread_blocks(block, dim, axis):
    half = block.shape[dim] // 2
    held = {0: block}
    pieces = {0: [(0, block)]}
    order = sorted(range(1, lax.axis_size(axis)), key=lambda k: (k.bit_count(), k))
    for k in order:
        low = k & -k
        high = 1 << (k.bit_length() - 1)
        if low == high:
            held[k] = flipped(block, axis, k)
            pieces[k] = [(0, held[k])]
        else:
            first = lax.slice_in_dim(held[k ^ low], 0, half, axis=dim)
            second = lax.slice_in_dim(held[k ^ high], half, 2 * half, axis=dim)
            first, second = flipped(first, axis, low), flipped(second, axis, high)
            pieces[k] = [(0, first), (half, second)]
            if k.bit_count() < lax.axis_size(axis).bit_length() - 1:
                held[k] = lax.concatenate([first, second], dim)
    return pieces, held


def chain_step(value, moves):
    return lax.ppermute(
        value, "col", [(2 * a + core, 2 * b + core) for a, b in moves for core in range(2)]
    )


def gather_chain(hidden):
    chips = lax.axis_size("col") // 2
    chip = lax.axis_index("col") // 2
    blocks = [(chip, hidden, flipped(hidden, "col", 1))]
    upward = downward = hidden
    for step in range(1, chips):
        up = [(a, a + 1) for a in range(step - 1, chips - 1)]
        down = [(a, a - 1) for a in range(1, chips - step + 1)]
        if 2 * step > chips + 1:
            owns, mains, others = zip(*blocks)
            swapped = others[: -1]
            upward, *swapped = lax.optimization_barrier((upward, *swapped))
            blocks = list(zip(owns, mains, [*swapped, *others[-1:]]))
            upward = downward = chain_step(upward, up + down)
        else:
            upward, downward = chain_step(upward, up), chain_step(downward, down)
            if 2 * step > chips - 1:
                upward = downward = jnp.where(chip >= step, upward, downward)
        if 2 * step > chips - 1:
            owner = jnp.where(chip >= step, chip - step, jnp.minimum(chip + step, chips - 1))
            swapped = flipped(upward, "col", 1) if step < chips - 1 else None
            blocks.append((owner, upward, swapped))
        else:
            for owner, block in ((chip - step, upward), (chip + step, downward)):
                swapped = flipped(block, "col", 1) if step < chips - 1 else None
                blocks.append((jnp.clip(owner, 0, chips - 1), block, swapped))
    return blocks


def on_device(state, noise, mod_shift, mod_scale, mod_gate, w_in, b_in, w_out, b_out):
    row = lax.axis_index("row")
    core = lax.axis_index("col") % 2
    in_pieces, _ = spread_blocks(w_in, 0, "row")
    sums = jnp.stack((jnp.sum(state, axis=0), jnp.sum(state * state, axis=0)))
    bits = 1
    while bits < lax.axis_size("col"):
        sums = sums + flipped(sums, "col", bits)
        bits *= 2
    center = sums[0] / D
    spread = sums[1] / D - center * center
    normed = (
        (state - center[None, :]) * lax.rsqrt(spread[None, :] + 1e-06) * (1.0 + mod_scale[:, None])
        + mod_shift[:, None]
    ).astype(jnp.bfloat16)
    normed_all = lax.all_gather(normed, "col", axis=0, tiled=True)

    tokens = state.shape[1]
    spans = [(0, tokens // 2), (tokens // 2, tokens)]
    chains = []
    for lo, hi in spans:
        pre_act = None
        for k, parts in in_pieces.items():
            if k and len(parts) > 1:
                pre_act, *arrived = lax.optimization_barrier((pre_act, *[piece for _, piece in parts]))
                parts = [(offset, piece) for (offset, _), piece in zip(parts, arrived)]
            for offset, piece in parts:
                start = (row ^ k) * w_in.shape[0] + offset
                part = lax.dynamic_slice(normed_all, (start, lo), (piece.shape[0], hi - lo))
                term = lax.dot_general(
                    piece, part, (((0,), (0,)), ((), ())), preferred_element_type=jnp.float32
                )
                pre_act = term if pre_act is None else pre_act + term
        hidden = jax.nn.gelu(pre_act + b_in[:, None], approximate=True).astype(jnp.bfloat16)
        chains.append(gather_chain(hidden))
    w_out, _ = lax.optimization_barrier((w_out, piece))
    w_out_all = lax.all_gather(w_out, "row", axis=1, tiled=True)


    halves = []
    for blocks in chains:
        mixed_out = None
        units = w_in.shape[1]
        for owner, block, swapped in blocks:
            if swapped is None:
                block, mixed_out = lax.optimization_barrier((block, mixed_out))
                swapped = flipped(block, "col", 1)
            for near, value in ((core, block), (1 - core, swapped)):
                weights = lax.dynamic_slice_in_dim(w_out_all, (2 * owner + near) * units, units, axis=1)
                term = jnp.dot(weights, value, preferred_element_type=jnp.float32)
                mixed_out = term if mixed_out is None else mixed_out + term
        halves.append(mixed_out)
    mixed_out = lax.concatenate(halves, 1)
    branch = mixed_out + b_out[:, None]
    predicted = state + mod_gate[:, None] * branch
    purified = (
        state * (1.0 + 0.5 * beta_now * step_width)
        - beta_now * step_width / sigma_now * predicted
        + math.sqrt(beta_now * step_width) * noise
    )
    return (purified, predicted)


def solution(mesh):
    in_specs = (
        P("col", "row"),
        P("col", "row"),
        P("col"),
        P("col"),
        P("col"),
        P("row", "col"),
        P("col"),
        P("col", "row"),
        P("col"),
    )
    out_specs = (P("col", "row"), P("col", "row"))
    return jax.shard_map(
        on_device, mesh=mesh, in_specs=in_specs, out_specs=out_specs, check_vma=False
    )
```

```python
import math

import jax
import jax.numpy as jnp
from jax import lax
from jax.sharding import PartitionSpec as P

D = 3072


beta_now = 2.09
step_width = 0.02
sigma_now = 0.322


def flipped(value, axis, bits):
    devices = lax.axis_size(axis)
    return lax.ppermute(value, axis, [(i, i ^ bits) for i in range(devices)])


def spread_blocks(block, dim, axis):
    half = block.shape[dim] // 2
    held = {0: block}
    pieces = {0: [(0, block)]}
    order = sorted(range(1, lax.axis_size(axis)), key=lambda k: (k.bit_count(), k))
    for k in order:
        low = k & -k
        high = 1 << (k.bit_length() - 1)
        if low == high:
            held[k] = flipped(block, axis, k)
            pieces[k] = [(0, held[k])]
        else:
            first = lax.slice_in_dim(held[k ^ low], 0, half, axis=dim)
            second = lax.slice_in_dim(held[k ^ high], half, 2 * half, axis=dim)
            first, second = flipped(first, axis, low), flipped(second, axis, high)
            pieces[k] = [(0, first), (half, second)]
            if k.bit_count() < lax.axis_size(axis).bit_length() - 1:
                held[k] = lax.concatenate([first, second], dim)
    return pieces, held


def chain_step(value, moves):
    return lax.ppermute(
        value, "col", [(2 * a + core, 2 * b + core) for a, b in moves for core in range(2)]
    )


def gather_chain(hidden):
    chips = lax.axis_size("col") // 2
    chip = lax.axis_index("col") // 2
    blocks = [(chip, hidden, flipped(hidden, "col", 1))]
    upward = downward = hidden
    for step in range(1, chips):
        up = [(a, a + 1) for a in range(step - 1, chips - 1)]
        down = [(a, a - 1) for a in range(1, chips - step + 1)]
        if 2 * step > chips + 1:
            owns, mains, others = zip(*blocks)
            swapped = others[: -1]
            upward, *swapped = lax.optimization_barrier((upward, *swapped))
            blocks = list(zip(owns, mains, [*swapped, *others[-1:]]))
            upward = downward = chain_step(upward, up + down)
        else:
            upward, downward = chain_step(upward, up), chain_step(downward, down)
            if 2 * step > chips - 1:
                upward = downward = jnp.where(chip >= step, upward, downward)
        if 2 * step > chips - 1:
            owner = jnp.where(chip >= step, chip - step, jnp.minimum(chip + step, chips - 1))
            swapped = flipped(upward, "col", 1) if step < chips - 1 else None
            blocks.append((owner, upward, swapped))
        else:
            for owner, block in ((chip - step, upward), (chip + step, downward)):
                swapped = flipped(block, "col", 1) if step < chips - 1 else None
                blocks.append((jnp.clip(owner, 0, chips - 1), block, swapped))
    return blocks


def on_device(state, noise, mod_shift, mod_scale, mod_gate, w_in, b_in, w_out, b_out):
    row = lax.axis_index("row")
    core = lax.axis_index("col") % 2
    in_pieces, _ = spread_blocks(w_in, 0, "row")
    sums = jnp.stack((jnp.sum(state, axis=0), jnp.sum(state * state, axis=0)))
    bits = 1
    while bits < lax.axis_size("col"):
        sums = sums + flipped(sums, "col", bits)
        bits *= 2
    center = sums[0] / D
    spread = sums[1] / D - center * center
    normed = (
        (state - center[None, :]) * lax.rsqrt(spread[None, :] + 1e-06) * (1.0 + mod_scale[:, None])
        + mod_shift[:, None]
    ).astype(jnp.bfloat16)
    normed_all = lax.all_gather(normed, "col", axis=0, tiled=True)

    tokens = state.shape[1]
    cut = tokens * 2 // 3 if tokens % 384 == 0 else tokens // 2
    spans = [(0, cut), (cut, tokens)]
    chains = []
    for lo, hi in spans:
        pre_act = None
        for k, parts in in_pieces.items():
            if k and len(parts) > 1:
                pre_act, *arrived = lax.optimization_barrier((pre_act, *[piece for _, piece in parts]))
                parts = [(offset, piece) for (offset, _), piece in zip(parts, arrived)]
            for offset, piece in parts:
                start = (row ^ k) * w_in.shape[0] + offset
                part = lax.dynamic_slice(normed_all, (start, lo), (piece.shape[0], hi - lo))
                term = lax.dot_general(
                    piece, part, (((0,), (0,)), ((), ())), preferred_element_type=jnp.float32
                )
                pre_act = term if pre_act is None else pre_act + term
        hidden = jax.nn.gelu(pre_act + b_in[:, None], approximate=True).astype(jnp.bfloat16)
        chains.append(gather_chain(hidden))
    w_out, _ = lax.optimization_barrier((w_out, piece))
    w_out_all = lax.all_gather(w_out, "row", axis=1, tiled=True)


    halves = []
    for blocks in chains:
        mixed_out = None
        units = w_in.shape[1]
        for owner, block, swapped in blocks:
            if swapped is None:
                block, mixed_out = lax.optimization_barrier((block, mixed_out))
                swapped = flipped(block, "col", 1)
            for near, value in ((core, block), (1 - core, swapped)):
                weights = lax.dynamic_slice_in_dim(w_out_all, (2 * owner + near) * units, units, axis=1)
                term = jnp.dot(weights, value, preferred_element_type=jnp.float32)
                mixed_out = term if mixed_out is None else mixed_out + term
        halves.append(mixed_out)
    mixed_out = lax.concatenate(halves, 1)
    branch = mixed_out + b_out[:, None]
    predicted = state + mod_gate[:, None] * branch
    purified = (
        state * (1.0 + 0.5 * beta_now * step_width)
        - beta_now * step_width / sigma_now * predicted
        + math.sqrt(beta_now * step_width) * noise
    )
    return (purified, predicted)


def solution(mesh):
    in_specs = (
        P("col", "row"),
        P("col", "row"),
        P("col"),
        P("col"),
        P("col"),
        P("row", "col"),
        P("col"),
        P("col", "row"),
        P("col"),
    )
    out_specs = (P("col", "row"), P("col", "row"))
    return jax.shard_map(
        on_device, mesh=mesh, in_specs=in_specs, out_specs=out_specs, check_vma=False
    )
```
